32 devices in a mesh: leaf: 4 (over y, x), col: 8 (over z, core).
Axes of the slice: x: 2, y: 2, z: 4, core: 2. Of those that a mesh axis runs over, the one named last changes fastest.
Arguments:
- right_sides: bfloat16 [4, 2, 1792, 128], P('leaf', None, 'col'), may hold values from -6 to 6
- leaf_inverse: bfloat16 [4, 1792, 1792], P('leaf', 'col'), as said below
- upper_inverse: bfloat16 [4, 1792, 1792], P('leaf', 'col'), as said below
- leaf_update: bfloat16 [4, 4, 1792, 512], P('leaf', None, 'col'), may hold values from -0.0625 to 0.0625
- upper_update: bfloat16 [4, 4, 1792, 512], P('leaf', None, 'col'), may hold values from -0.0625 to 0.0625
- live_rows: int32 [4, 2], P('leaf'), may hold values from 896 to 1792, as said below
- tile_map: int32 [4, 2, 4, 512], P('leaf'), may hold values from 0 to 1791, as said below
Outputs:
- solution: bfloat16 [4, 2, 1792, 128], P('leaf', None, 'col')
The draws below stay inside these ranges and needn't reach their ends.
Inputs may be any that keep to these rules, and one draw needn't show every extreme that they name: `leaf_inverse`: zero above the diagonal, nonzero on it. `upper_inverse`: zero above the diagonal, nonzero on it. `live_rows`: one supernode has all 1792 rows live and one has 896. `tile_map`: the rows of one tile are distinct and increasing.
All inputs are finite; a program needn't handle non-finite values.
Results may differ from the reference program's by a relative error of at most 0.0075.
Values may be sent and summed in bfloat16 or wider, within the bound.
A program may use at most 64 MiB of HBM per device.

```python
import jax
import jax.numpy as jnp
from jax import lax

SN = 1792
TILE = 512
ANC = 4
RHS = 128
N_LEAF = 4


def draw_triangle(key):
    first_key, second_key = jax.random.split(key)
    shape = (N_LEAF, SN, SN)
    row_ids = lax.broadcasted_iota(jnp.int32, (1, SN, SN), 1)
    col_ids = lax.broadcasted_iota(jnp.int32, (1, SN, SN), 2)
    diagonal = jax.random.uniform(first_key, (N_LEAF, SN, 1), jnp.float32, 0.6, 1.4)
    lower = jax.random.normal(second_key, shape, jnp.float32) * (0.5 / SN ** 0.5)
    zeros = jnp.zeros(shape, jnp.float32)
    result = jnp.where(row_ids == col_ids, diagonal, jnp.where(col_ids < row_ids, lower, zeros))
    return result.astype(jnp.bfloat16)


def draw_leaf_inverse(key, part):
    return draw_triangle(jax.random.fold_in(key, 11))


def draw_upper_inverse(key, part):
    return draw_triangle(jax.random.fold_in(key, 12))


def draw_live_rows(key, part):
    first_key, second_key, third_key = jax.random.split(jax.random.fold_in(key, 13), 3)
    total = N_LEAF * 2
    sizes = jax.random.randint(first_key, (total,), SN // 2, SN + 1, jnp.int32)
    place_full = jax.random.randint(second_key, (), 0, total, jnp.int32)
    place_half = (place_full + 1 + jax.random.randint(third_key, (), 0, total - 1, jnp.int32)) % total
    sizes = sizes.at[place_full].set(SN)
    sizes = sizes.at[place_half].set(SN // 2)
    return sizes.reshape(N_LEAF, 2)


def draw_tile_map(key, part):
    keys = jax.random.split(jax.random.fold_in(key, 14), N_LEAF * 2 * ANC)

    def one_tile(tile_key):
        return jnp.sort(jax.random.permutation(tile_key, SN)[:TILE]).astype(jnp.int32)
    return jax.vmap(one_tile)(keys).reshape(N_LEAF, 2, ANC, TILE)


def block_scale(rng, dims, cuts, least, high):
    def one(axis_at, shards_of):
        heights = jax.random.uniform(jax.random.fold_in(jax.random.fold_in(rng, 6), axis_at), (shards_of,), jnp.float32, least / len(cuts), high / len(cuts))
        return jnp.repeat(jnp.exp(heights), dims[axis_at] // shards_of).reshape((-1,) + (1,) * (len(dims) - axis_at - 1))

    loudness = one(*cuts[0])
    for cut in cuts[1:]:
        loudness = loudness * one(*cut)
    return loudness


def noise(own_key, shape, width, most, shards=(), kind=jnp.bfloat16):
    gain = block_scale(own_key, shape, shards, -0.22, 0.18) if shards else 1.0
    values = jax.random.normal(own_key, shape, jnp.float32) * width * gain
    return jnp.minimum(jnp.maximum(values, -most), most).astype(kind)


def setup_inputs(seed: int = 0) -> dict:
    key_list = jax.random.split(jax.random.key(seed), 8)
    return {
        "right_sides": noise(key_list[0], (N_LEAF, 2, SN, RHS), 1.0, 6.0, ((0, 4), (2, 8))),
        "leaf_inverse": draw_leaf_inverse(jax.random.fold_in(key_list[7], 71), 0),
        "upper_inverse": draw_upper_inverse(jax.random.fold_in(key_list[7], 71), 0),
        "leaf_update": noise(key_list[3], (N_LEAF, ANC, SN, TILE), (4 * SN) ** -0.5, 0.0625, ((0, 4), (2, 8))),
        "upper_update": noise(key_list[4], (N_LEAF, ANC, SN, TILE), (4 * SN) ** -0.5, 0.0625, ((0, 4), (2, 8))),
        "live_rows": draw_live_rows(jax.random.fold_in(key_list[7], 71), 0),
        "tile_map": draw_tile_map(jax.random.fold_in(key_list[7], 71), 0),
    }


def reference(right_sides, leaf_inverse, upper_inverse, leaf_update, upper_update, live_rows, tile_map):
    depth = N_LEAF.bit_length() - 1
    row_ids = jnp.arange(SN, dtype=jnp.int32)

    def row_mask(node, which):
        return (row_ids < live_rows[node, which]).astype(jnp.float32)[:, None]

    def level_of(node):
        return (node & -node).bit_length()

    def ancestor(node, height):
        return ((node >> height) << height) + (1 << (height - 1))

    def forward_solve(inverse, residual, masking):
        shares = (residual * masking).astype(jnp.bfloat16)
        return (jnp.dot(inverse, shares, preferred_element_type=jnp.float32) * masking).astype(jnp.bfloat16)

    def backward_solve(inverse, solved, pulled, masking):
        scaled = ((solved.astype(jnp.float32) - pulled) * masking).astype(jnp.bfloat16)
        return (jnp.dot(inverse.T, scaled, preferred_element_type=jnp.float32) * masking).astype(jnp.bfloat16)

    residual_up = {}
    for node in range(1, N_LEAF):
        residual_up[node] = right_sides[node, 1].astype(jnp.float32)

    def push(target, tile_rows, update, solved):
        residual_up[target] = residual_up[target].at[tile_rows].add(
            -jnp.dot(update.T, solved, preferred_element_type=jnp.float32))

    solved_leaf = {}
    for node in range(N_LEAF):
        solved = forward_solve(leaf_inverse[node], right_sides[node, 0].astype(jnp.float32), row_mask(node, 0))
        solved_leaf[node] = solved
        for slot_idx in range(depth):
            push(ancestor(node, slot_idx + 1), tile_map[node, 0, slot_idx], leaf_update[node, slot_idx], solved)

    solved_up = {}
    for height in range(1, depth + 1):
        for node in range(1, N_LEAF):
            if level_of(node) == height:
                solved = forward_solve(upper_inverse[node], residual_up[node], row_mask(node, 1))
                solved_up[node] = solved
                for slot_idx in range(depth - height):
                    push(ancestor(node, height + 1 + slot_idx), tile_map[node, 1, slot_idx], upper_update[node, slot_idx], solved)

    answer_up = {}
    for height in range(depth, 0, -1):
        for node in range(1, N_LEAF):
            if level_of(node) == height:
                pulled = jnp.zeros((SN, RHS), jnp.float32)
                for slot_idx in range(depth - height):
                    upper_x = answer_up[ancestor(node, height + 1 + slot_idx)]
                    picked = upper_x[tile_map[node, 1, slot_idx]]
                    pulled = pulled + jnp.dot(upper_update[node, slot_idx], picked, preferred_element_type=jnp.float32)
                answer_up[node] = backward_solve(upper_inverse[node], solved_up[node], pulled, row_mask(node, 1))

    blocks = []
    for node in range(N_LEAF):
        pulled = jnp.zeros((SN, RHS), jnp.float32)
        for slot_idx in range(depth):
            upper_x = answer_up[ancestor(node, slot_idx + 1)]
            picked = upper_x[tile_map[node, 0, slot_idx]]
            pulled = pulled + jnp.dot(leaf_update[node, slot_idx], picked, preferred_element_type=jnp.float32)
        answer_leaf = backward_solve(leaf_inverse[node], solved_leaf[node], pulled, row_mask(node, 0))
        if node == 0:
            answer_top = jnp.zeros((SN, RHS), jnp.bfloat16)
        else:
            answer_top = answer_up[node]
        blocks.append(jnp.stack([answer_leaf, answer_top]))
    return jnp.stack(blocks)
```

```python
import functools

import jax
import jax.numpy as jnp
from jax import lax
from jax.experimental import pallas as pl
from jax.experimental.pallas import tpu as pltpu
from jax.sharding import PartitionSpec as P

MESH = pl.DeviceIdType.MESH
F32 = jnp.float32
BF16 = jnp.bfloat16


def dot(a, b, ca, cb):
    return lax.dot_general(a, b, (((ca,), (cb,)), ((), ())), preferred_element_type=F32)


def kernel(
    nl, nc, depth, anc, rs, linv, uinv, lupd, uupd, live, map_in, out,
    maps, rbuf, bbuf, xb, wl, wu, z_all, tiles, ylbuf, yubuf, lt, ut, b_sum, g_sum,
    a1, a2, a3, a4, b1, b2, b3, b4, c1, c2, c3, c4, d1, d2, d3, d4,
    map_send, map_recv, ag_send, ag_fwd, ag_recv, p_send, p_recv, q_send, q_recv,
    t_send, t_fwd, t_recv, x_send, x_recv,
):
    rows, sn = linv.shape
    width = rs.shape[2]
    tile = map_in.shape[1]
    chunk = tile // nc
    half = nc // 2
    leaf = lax.axis_index("leaf")
    col = lax.axis_index("col")
    par = lax.rem(col, 2)
    z = lax.div(col, 2)
    sib = col + 1 - 2 * par
    level = jnp.int32(0)
    for k in range(depth):
        level = level + jnp.where((lax.rem(leaf, 2**k) == 0) & (leaf > 0), 1, 0)

    def base_of(h):
        return lax.div(leaf, 2**h) * 2**h

    def owner(h):
        return base_of(h) + 2 ** (h - 1)

    def rc(src, dst, send, recv, where, at=None):
        return pltpu.make_async_remote_copy(
            src_ref=src, dst_ref=dst, send_sem=send, recv_sem=recv,
            device_id=(leaf if at is None else at, where), device_id_type=MESH,
        )

    def got(ref, sem):
        rc(ref, ref, sem, sem, sib).wait_recv()

    def sent(ref, sem):
        rc(ref, ref, sem, sem, sib).wait_send()

    row_ids = col * rows + lax.broadcasted_iota(jnp.int32, (rows, width), 0)
    leaf_mask = row_ids < live[0, 0]
    upper_mask = row_ids < live[0, 1]

    def ag_start(use, buf):
        for k in range(1, half):
            to = 2 * lax.rem(z + k, half) + par
            rc(buf.at[col], buf.at[col], ag_send.at[use, k], ag_recv.at[use, col], to).start()
        rc(buf.at[col], buf.at[col], ag_send.at[use, 0], ag_recv.at[use, col], sib).start()

    def ag_forward(use, buf):
        for k in range(1, half):
            src = 2 * lax.rem(z - k + half, half) + par
            got(buf.at[src], ag_recv.at[use, src])
            rc(buf.at[src], buf.at[src], ag_fwd.at[use, k], ag_recv.at[use, src], sib).start()

    def ag_finish(use, buf):
        for zz in range(half):
            src = 2 * zz + 1 - par
            got(buf.at[src], ag_recv.at[use, src])

    def ag_sent(use, buf):
        for k in range(half):
            sent(buf.at[col], ag_send.at[use, k])
        for k in range(1, half):
            sent(buf.at[col], ag_fwd.at[use, k])

    def reduce(use, bufs, count):
        s1, r1, s2, r2 = bufs
        n = pl.ds(0, count)
        rc(s1.at[1 - par, :, n], r1.at[:, n], p_send.at[use], p_recv.at[use], sib).start()
        got(r1.at[:, n], p_recv.at[use])
        for k in range(1, half):
            zz = lax.rem(z + k, half)
            s2[k, n] = (s1[par, zz, n].astype(F32) + r1[zz, n].astype(F32)).astype(BF16)
            rc(s2.at[k, n], r2.at[k, n], q_send.at[use, k], q_recv.at[use, k], 2 * zz + par).start()
        total = s1[par, z, n].astype(F32) + r1[z, n].astype(F32)
        for k in range(1, half):
            got(r2.at[k, n], q_recv.at[use, k])
            total = total + r2[k, n].astype(F32)
        return total

    def reduce_sent(use, bufs, count):
        s1, r1, s2, r2 = bufs
        n = pl.ds(0, count)
        sent(r1.at[:, n], p_send.at[use])
        for k in range(1, half):
            sent(s2.at[k, n], q_send.at[use, k])

    def tile_parts(upd, slots, y, bufs):
        for s in range(slots):
            part = dot(upd[s], y, 0, 0).astype(BF16)
            for j in range(nc):
                bufs[0][j % 2, j // 2, s * chunk:(s + 1) * chunk] = part[j * chunk:(j + 1) * chunk]

    def send_chunks(which, held, first, slots):
        for s in range(slots):
            to = owner(first + s)
            for zz in range(half):

                @pl.when((to != leaf) | (z != zz))
                def _():
                    rc(held.at[s], tiles.at[which, leaf, col], t_send.at[which, s, zz],
                       t_recv.at[which, leaf, col], 2 * zz + par, to).start()

            @pl.when(to == leaf)
            def _():
                tiles[which, leaf, col] = held[s]

    def chunks_sent(which, held, first, slots):
        for s in range(slots):
            to = owner(first + s)
            for zz in range(half):

                @pl.when((to != leaf) | (z != zz))
                def _():
                    sent(held.at[s], t_send.at[which, s, zz])

    def onehot(row):
        ids = lax.broadcasted_iota(jnp.int32, (sn, tile), 0)
        return jnp.where(ids == row, 1.0, 0.0).astype(BF16)

    rbuf[col] = jnp.where(leaf_mask, rs[0].astype(F32), 0.0).astype(BF16)
    ag_start(0, rbuf)
    bbuf[col] = jnp.where(upper_mask, rs[1].astype(F32), 0.0).astype(BF16)
    ag_start(1, bbuf)
    maps[leaf] = map_in[...]
    for k in range(1, nl):
        rc(maps.at[leaf], maps.at[leaf], map_send.at[k], map_recv.at[leaf], col, lax.rem(leaf + k, nl)).start()
    ag_forward(0, rbuf)
    for s in range(depth):
        wl[s] = dot(lupd[s], onehot(map_in[s:s + 1]), 1, 1).astype(BF16)
    ag_finish(0, rbuf)
    solved = dot(linv[...], rbuf[...].reshape(sn, width), 1, 0)
    ylbuf[...] = jnp.where(leaf_mask, solved, 0.0).astype(BF16)
    bufs_a, bufs_b, bufs_c, bufs_d = (a1, a2, a3, a4), (b1, b2, b3, b4), (c1, c2, c3, c4), (d1, d2, d3, d4)
    tile_parts(lupd, depth, ylbuf[...], bufs_a)
    lt[...] = reduce(0, bufs_a, depth * chunk).reshape(depth, chunk, width).astype(BF16)
    send_chunks(0, lt, 1, depth)
    ag_forward(1, bbuf)
    for k in range(1, nl):
        src = lax.rem(leaf - k + nl, nl)
        got(maps.at[src], map_recv.at[src])
    ag_finish(1, bbuf)
    yubuf[...] = jnp.zeros((rows, width), F32).astype(BF16)

    for h in range(1, depth + 1):

        @pl.when(level == h)
        def _():
            first = base_of(h)
            slots = depth - h

            def level_in(i):
                out_level = jnp.int32(0)
                for k in range(depth):
                    out_level = out_level + jnp.where((lax.rem(i, 2**k) == 0) & (i > 0), 1, 0)
                return out_level

            def each(fn):
                def leaf_body(i, _):
                    fn(0, first + i, h - 1)
                    return 0

                lax.fori_loop(0, 2**h, leaf_body, 0)
                if h > 1:

                    def upper_body(i, _):
                        @pl.when(i != 2 ** (h - 1))
                        def _():
                            fn(1, first + i, anc + h - level_in(i) - 1)

                        return 0

                    lax.fori_loop(1, 2**h, upper_body, 0)

            def prepare(which, src, slot):
                row = maps[src, pl.ds(slot, 1), :]
                row = jnp.where(row < live[0, 1], row, -1)
                z_all[which, src] = dot(uinv[...], onehot(row), 1, 0).astype(BF16)

            each(prepare)
            for s in range(slots):
                wu[s] = dot(uupd[s], onehot(map_in[anc + s:anc + s + 1]), 1, 1).astype(BF16)
            b_sum[...] = dot(uinv[...], bbuf[...].reshape(sn, width), 1, 0)

            def pass_on(which, src, slot):
                for zz in range(half):
                    c = 2 * zz + par

                    @pl.when((src != leaf) | (zz != z))
                    def _():
                        got(tiles.at[which, src, c], t_recv.at[which, src, c])

                    rc(tiles.at[which, src, c], tiles.at[which, src, c], t_fwd.at[which, src, zz],
                       t_recv.at[which, src, c], sib).start()

            def take(which, src, slot):
                for zz in range(half):
                    c = 2 * zz + 1 - par
                    got(tiles.at[which, src, c], t_recv.at[which, src, c])
                b_sum[...] -= dot(z_all[which, src], tiles[which, src].reshape(tile, width), 1, 0)

            each(pass_on)
            each(take)
            yubuf[...] = jnp.where(upper_mask, b_sum[...], 0.0).astype(BF16)
            if slots > 0:
                tile_parts(uupd, slots, yubuf[...], bufs_b)
                ut[pl.ds(0, slots)] = reduce(1, bufs_b, slots * chunk).reshape(slots, chunk, width).astype(BF16)
                send_chunks(1, ut, h + 1, slots)

            def fwd_sent(which, src, slot):
                for zz in range(half):
                    sent(tiles.at[which, src, zz], t_fwd.at[which, src, zz])

            each(fwd_sent)

    def back(inv, y, g, mask, use, bufs):
        v = jnp.where(mask, y.astype(F32) - g, 0.0).astype(BF16)
        part = dot(inv[...], v, 0, 0).astype(BF16)
        for j in range(nc):
            bufs[0][j % 2, j // 2] = part[j * rows:(j + 1) * rows]
        return jnp.where(mask, reduce(use, bufs, rows), 0.0).astype(BF16)

    out[1] = jnp.zeros((rows, width), F32).astype(BF16)
    g_sum[...] = jnp.zeros((rows, width), F32)
    for h in range(depth, 0, -1):
        buf = xb.at[h - 1]

        @pl.when(level == h)
        def _():
            g = jnp.zeros((rows, width), F32)
            for s in range(depth - h):
                g = g + dot(wu[s], xb[h + s].reshape(sn, width), 1, 0)
            x = back(uinv, yubuf[...], g, upper_mask, 2, bufs_c)
            buf[col] = x
            for k in range(1, 2**h):
                to = base_of(h) + lax.rem(leaf - base_of(h) + k, 2**h)
                rc(buf.at[col], buf.at[col], x_send.at[h - 1, k], x_recv.at[h - 1], col, to).start()
            out[1] = x

        @pl.when(level != h)
        def _():
            got(buf.at[col], x_recv.at[h - 1])

        ag_start(1 + h, buf)
        ag_forward(1 + h, buf)
        ag_finish(1 + h, buf)
        if h > 1:
            g_sum[...] += dot(wl[h - 1], xb[h - 1].reshape(sn, width), 1, 0)
    g = g_sum[...] + dot(wl[0], xb[0].reshape(sn, width), 1, 0)
    out[0] = back(linv, ylbuf[...], g, leaf_mask, 3, bufs_d)

    for k in range(1, nl):
        sent(maps.at[leaf], map_send.at[k])
    ag_sent(0, rbuf)
    ag_sent(1, bbuf)
    reduce_sent(0, bufs_a, depth * chunk)
    reduce_sent(3, bufs_d, rows)
    chunks_sent(0, lt, 1, depth)
    for h in range(1, depth + 1):
        buf = xb.at[h - 1]
        ag_sent(1 + h, buf)

        @pl.when(level == h)
        def _():
            for k in range(1, 2**h):
                sent(buf.at[col], x_send.at[h - 1, k])
            reduce_sent(2, bufs_c, rows)
            if depth > h:
                reduce_sent(1, bufs_b, (depth - h) * chunk)
                chunks_sent(1, ut, h + 1, depth - h)


def shards(right_sides, leaf_inverse, upper_inverse, leaf_update, upper_update, live_rows, tile_map):
    nl, nc = lax.axis_size("leaf"), lax.axis_size("col")
    depth = nl.bit_length() - 1
    _, rows, sn = leaf_inverse.shape
    width = right_sides.shape[3]
    anc, tile = tile_map.shape[2:]
    half, chunk = nc // 2, tile // nc
    up = max(depth - 1, 1)
    vm = lambda *shape: pltpu.VMEM(shape, BF16)
    four = lambda n: [vm(2, half, n, width)] + [vm(half, n, width)] * 3
    dma = lambda *shape: pltpu.SemaphoreType.DMA(shape)
    whole = pl.BlockSpec(memory_space=pltpu.VMEM)
    answer = pl.pallas_call(
        functools.partial(kernel, nl, nc, depth, anc),
        out_shape=jax.ShapeDtypeStruct((2, rows, width), BF16),
        in_specs=[whole] * 5 + [pl.BlockSpec(memory_space=pltpu.SMEM), whole],
        out_specs=whole,
        scratch_shapes=[
            pltpu.VMEM((nl, 2 * anc, tile), jnp.int32),
            vm(nc, rows, width), vm(nc, rows, width), vm(depth, nc, rows, width),
            vm(depth, rows, sn), vm(up, rows, sn), vm(2, nl, rows, tile),
            vm(2, nl, nc, chunk, width), vm(rows, width), vm(rows, width),
            vm(depth, chunk, width), vm(up, chunk, width),
            pltpu.VMEM((rows, width), F32), pltpu.VMEM((rows, width), F32),
            *four(depth * chunk), *four(up * chunk), *four(rows), *four(rows),
            dma(nl), dma(nl),
            dma(depth + 2, half), dma(depth + 2, half), dma(depth + 2, nc),
            dma(4), dma(4), dma(4, half), dma(4, half),
            dma(2, depth, half), dma(2, nl, half), dma(2, nl, nc),
            dma(depth, nl), dma(depth),
        ],
        compiler_params=pltpu.CompilerParams(has_side_effects=True, vmem_limit_bytes=48 * 1024 * 1024),
    )(
        right_sides[0], leaf_inverse[0], upper_inverse[0], leaf_update[0], upper_update[0],
        live_rows, tile_map[0].reshape(2 * anc, tile),
    )
    return answer[None]


def solution(mesh):
    placed = (
        P("leaf", None, "col", None),
        P("leaf", "col", None),
        P("leaf", "col", None),
        P("leaf", None, "col", None),
        P("leaf", None, "col", None),
        P("leaf", None),
        P("leaf", None, None, None),
    )
    return jax.shard_map(
        shards, mesh=mesh, in_specs=placed, out_specs=P("leaf", None, "col", None), check_vma=False
    )
```

```python
import functools

import jax
import jax.numpy as jnp
from jax import lax
from jax.experimental import pallas as pl
from jax.experimental.pallas import tpu as pltpu
from jax.sharding import PartitionSpec as P

MESH = pl.DeviceIdType.MESH
F32 = jnp.float32
BF16 = jnp.bfloat16


def dot(a, b, ca, cb):
    return lax.dot_general(a, b, (((ca,), (cb,)), ((), ())), preferred_element_type=F32)


def kernel(
    nl, nc, depth, anc, rs, linv_in, uinv_in, lupd_in, uupd_in, live, map_in, out,
    linv, uinv, lupd, uupd, linv_t, uinv_t, lupd_t, uupd_t,
    maps, rbuf, bbuf, xb, wl, wu, z_all, tiles, ylbuf, yubuf, lt, ut, b_sum, g_sum,
    a1, a2, a3, a4, b1, b2, b3, b4, c1, c2, c3, c4, d1, d2, d3, d4,
    map_send, map_recv, ag_send, ag_fwd, ag_recv, p_send, p_recv, q_send, q_recv,
    t_send, t_fwd, t_recv, x_send, x_recv, in_sem,
):
    rows, sn = linv.shape
    width = rs.shape[2]
    tile = map_in.shape[1]
    chunk = tile // nc
    half = nc // 2
    leaf = lax.axis_index("leaf")
    col = lax.axis_index("col")
    par = lax.rem(col, 2)
    z = lax.div(col, 2)
    sib = col + 1 - 2 * par
    level = jnp.int32(0)
    for k in range(depth):
        level = level + jnp.where((lax.rem(leaf, 2**k) == 0) & (leaf > 0), 1, 0)

    def base_of(h):
        return lax.div(leaf, 2**h) * 2**h

    def owner(h):
        return base_of(h) + 2 ** (h - 1)

    def rc(src, dst, send, recv, where, at=None):
        return pltpu.make_async_remote_copy(
            src_ref=src, dst_ref=dst, send_sem=send, recv_sem=recv,
            device_id=(leaf if at is None else at, where), device_id_type=MESH,
        )

    def got(ref, sem):
        rc(ref, ref, sem, sem, sib).wait_recv()

    def sent(ref, sem):
        rc(ref, ref, sem, sem, sib).wait_send()

    row_ids = col * rows + lax.broadcasted_iota(jnp.int32, (rows, width), 0)
    leaf_mask = row_ids < live[0, 0]
    upper_mask = row_ids < live[0, 1]

    def ag_start(use, buf):
        for k in range(1, half):
            to = 2 * lax.rem(z + k, half) + par
            rc(buf.at[col], buf.at[col], ag_send.at[use, k], ag_recv.at[use, col], to).start()
        rc(buf.at[col], buf.at[col], ag_send.at[use, 0], ag_recv.at[use, col], sib).start()

    def ag_forward(use, buf):
        for k in range(1, half):
            src = 2 * lax.rem(z - k + half, half) + par
            got(buf.at[src], ag_recv.at[use, src])
            rc(buf.at[src], buf.at[src], ag_fwd.at[use, k], ag_recv.at[use, src], sib).start()

    def ag_finish(use, buf):
        for zz in range(half):
            src = 2 * zz + 1 - par
            got(buf.at[src], ag_recv.at[use, src])

    def ag_sent(use, buf):
        for k in range(half):
            sent(buf.at[col], ag_send.at[use, k])
        for k in range(1, half):
            sent(buf.at[col], ag_fwd.at[use, k])

    def reduce(use, bufs, count):
        s1, r1, s2, r2 = bufs
        n = pl.ds(0, count)
        rc(s1.at[1 - par, :, n], r1.at[:, n], p_send.at[use], p_recv.at[use], sib).start()
        got(r1.at[:, n], p_recv.at[use])
        for k in range(1, half):
            zz = lax.rem(z + k, half)
            s2[k, n] = (s1[par, zz, n].astype(F32) + r1[zz, n].astype(F32)).astype(BF16)
            rc(s2.at[k, n], r2.at[k, n], q_send.at[use, k], q_recv.at[use, k], 2 * zz + par).start()
        total = s1[par, z, n].astype(F32) + r1[z, n].astype(F32)
        for k in range(1, half):
            got(r2.at[k, n], q_recv.at[use, k])
            total = total + r2[k, n].astype(F32)
        return total

    def reduce_sent(use, bufs, count):
        s1, r1, s2, r2 = bufs
        n = pl.ds(0, count)
        sent(r1.at[:, n], p_send.at[use])
        for k in range(1, half):
            sent(s2.at[k, n], q_send.at[use, k])

    def tile_parts(upd, slots, y, bufs):
        for s in range(slots):
            part = dot(upd[s], y, 1, 0).astype(BF16)
            for j in range(nc):
                bufs[0][j % 2, j // 2, s * chunk:(s + 1) * chunk] = part[j * chunk:(j + 1) * chunk]

    def send_chunks(which, held, first, slots):
        for s in range(slots):
            to = owner(first + s)
            for zz in range(half):

                @pl.when((to != leaf) | (z != zz))
                def _():
                    rc(held.at[s], tiles.at[which, leaf, col], t_send.at[which, s, zz],
                       t_recv.at[which, leaf, col], 2 * zz + par, to).start()

            @pl.when(to == leaf)
            def _():
                tiles[which, leaf, col] = held[s]

    def chunks_sent(which, held, first, slots):
        for s in range(slots):
            to = owner(first + s)
            for zz in range(half):

                @pl.when((to != leaf) | (z != zz))
                def _():
                    sent(held.at[s], t_send.at[which, s, zz])

    def onehot(row):
        ids = lax.broadcasted_iota(jnp.int32, (sn, tile), 0)
        return jnp.where(ids == row, 1.0, 0.0).astype(BF16)

    def stage(h):
        first = base_of(h)

        def level_in(i):
            out_level = jnp.int32(0)
            for k in range(depth):
                out_level = out_level + jnp.where((lax.rem(i, 2**k) == 0) & (i > 0), 1, 0)
            return out_level

        def each(fn):
            def leaf_body(i, _):
                fn(0, first + i, h - 1)
                return 0

            lax.fori_loop(0, 2**h, leaf_body, 0)
            if h > 1:

                def upper_body(i, _):
                    @pl.when(i != 2 ** (h - 1))
                    def _():
                        fn(1, first + i, anc + h - level_in(i) - 1)

                    return 0

                lax.fori_loop(1, 2**h, upper_body, 0)

        def prepare(which, src, slot):
            row = maps[src, pl.ds(slot, 1), :]
            row = jnp.where(row < live[0, 1], row, -1)
            z_all[which, src] = dot(uinv[...], onehot(row), 1, 0).astype(BF16)

        return each, prepare

    up = wu.shape[0]
    loads = [
        pltpu.make_async_copy(lupd_in.at[pl.ds(0, depth)], lupd, in_sem.at[0]),
        pltpu.make_async_copy(uinv_in, uinv, in_sem.at[1]),
        pltpu.make_async_copy(linv_in, linv, in_sem.at[2]),
        pltpu.make_async_copy(uupd_in.at[pl.ds(0, up)], uupd, in_sem.at[3]),
    ]
    for load in loads:
        load.start()
    rbuf[col] = jnp.where(leaf_mask, rs[0].astype(F32), 0.0).astype(BF16)
    ag_start(0, rbuf)
    bbuf[col] = jnp.where(upper_mask, rs[1].astype(F32), 0.0).astype(BF16)
    ag_start(1, bbuf)
    maps[leaf] = map_in[...]
    for k in range(1, nl):
        rc(maps.at[leaf], maps.at[leaf], map_send.at[k], map_recv.at[leaf], col, lax.rem(leaf + k, nl)).start()
    ag_forward(0, rbuf)
    loads[0].wait()
    for s in range(depth):
        lupd_t[s] = lupd[s].T
    for k in range(1, nl):
        src = lax.rem(leaf - k + nl, nl)
        got(maps.at[src], map_recv.at[src])
    loads[1].wait()
    for h in range(1, depth):

        @pl.when(level == h)
        def _():
            each, prepare = stage(h)
            each(prepare)

    loads[2].wait()
    loads[3].wait()
    ag_finish(0, rbuf)
    solved = dot(linv[...], rbuf[...].reshape(sn, width), 1, 0)
    ylbuf[...] = jnp.where(leaf_mask, solved, 0.0).astype(BF16)
    bufs_a, bufs_b, bufs_c, bufs_d = (a1, a2, a3, a4), (b1, b2, b3, b4), (c1, c2, c3, c4), (d1, d2, d3, d4)
    tile_parts(lupd_t, depth, ylbuf[...], bufs_a)
    lt[...] = reduce(0, bufs_a, depth * chunk).reshape(depth, chunk, width).astype(BF16)
    send_chunks(0, lt, 1, depth)
    ag_forward(1, bbuf)
    ag_finish(1, bbuf)
    yubuf[...] = jnp.zeros((rows, width), F32).astype(BF16)

    for h in range(1, depth + 1):

        @pl.when(level == h)
        def _():
            slots = depth - h
            each, prepare = stage(h)
            if h == depth:
                each(prepare)
                uinv_t[...] = uinv[...].T
            for s in range(slots):
                uupd_t[s] = uupd[s].T
            b_sum[...] = dot(uinv[...], bbuf[...].reshape(sn, width), 1, 0)

            def pass_on(which, src, slot):
                for zz in range(half):
                    c = 2 * zz + par

                    @pl.when((src != leaf) | (zz != z))
                    def _():
                        got(tiles.at[which, src, c], t_recv.at[which, src, c])

                    rc(tiles.at[which, src, c], tiles.at[which, src, c], t_fwd.at[which, src, zz],
                       t_recv.at[which, src, c], sib).start()

            def take(which, src, slot):
                for zz in range(half):
                    c = 2 * zz + 1 - par
                    got(tiles.at[which, src, c], t_recv.at[which, src, c])
                b_sum[...] -= dot(z_all[which, src], tiles[which, src].reshape(tile, width), 1, 0)

            each(pass_on)
            each(take)
            yubuf[...] = jnp.where(upper_mask, b_sum[...], 0.0).astype(BF16)
            if slots > 0:
                tile_parts(uupd_t, slots, yubuf[...], bufs_b)
                ut[pl.ds(0, slots)] = reduce(1, bufs_b, slots * chunk).reshape(slots, chunk, width).astype(BF16)
                send_chunks(1, ut, h + 1, slots)
                for s in range(slots):
                    wu[s] = dot(uupd[s], onehot(map_in[anc + s:anc + s + 1]), 1, 1).astype(BF16)
                uinv_t[...] = uinv[...].T

            def fwd_sent(which, src, slot):
                for zz in range(half):
                    sent(tiles.at[which, src, zz], t_fwd.at[which, src, zz])

            each(fwd_sent)

    def back(inv, y, g, mask, use, bufs):
        v = jnp.where(mask, y.astype(F32) - g, 0.0).astype(BF16)
        part = dot(inv[...], v, 1, 0).astype(BF16)
        for j in range(nc):
            bufs[0][j % 2, j // 2] = part[j * rows:(j + 1) * rows]
        return jnp.where(mask, reduce(use, bufs, rows), 0.0).astype(BF16)

    out[1] = jnp.zeros((rows, width), F32).astype(BF16)
    g_sum[...] = jnp.zeros((rows, width), F32)

    def ready():
        linv_t[...] = linv[...].T
        for s in range(depth):
            wl[s] = dot(lupd[s], onehot(map_in[s:s + 1]), 1, 1).astype(BF16)

    pl.when(level != depth)(ready)
    for h in range(depth, 0, -1):
        buf = xb.at[h - 1]

        @pl.when(level == h)
        def _():
            g = jnp.zeros((rows, width), F32)
            for s in range(depth - h):
                g = g + dot(wu[s], xb[h + s].reshape(sn, width), 1, 0)
            x = back(uinv_t, yubuf[...], g, upper_mask, 2, bufs_c)
            buf[col] = x
            for k in range(1, 2**h):
                to = base_of(h) + lax.rem(leaf - base_of(h) + k, 2**h)
                rc(buf.at[col], buf.at[col], x_send.at[h - 1, k], x_recv.at[h - 1], col, to).start()
            out[1] = x

        @pl.when(level != h)
        def _():
            got(buf.at[col], x_recv.at[h - 1])

        ag_start(1 + h, buf)
        ag_forward(1 + h, buf)
        ag_finish(1 + h, buf)
        if h == depth:
            pl.when(level == depth)(ready)
        if h > 1:
            g_sum[...] += dot(wl[h - 1], xb[h - 1].reshape(sn, width), 1, 0)
    g = g_sum[...] + dot(wl[0], xb[0].reshape(sn, width), 1, 0)
    out[0] = back(linv_t, ylbuf[...], g, leaf_mask, 3, bufs_d)

    for k in range(1, nl):
        sent(maps.at[leaf], map_send.at[k])
    ag_sent(0, rbuf)
    ag_sent(1, bbuf)
    reduce_sent(0, bufs_a, depth * chunk)
    reduce_sent(3, bufs_d, rows)
    chunks_sent(0, lt, 1, depth)
    for h in range(1, depth + 1):
        buf = xb.at[h - 1]
        ag_sent(1 + h, buf)

        @pl.when(level == h)
        def _():
            for k in range(1, 2**h):
                sent(buf.at[col], x_send.at[h - 1, k])
            reduce_sent(2, bufs_c, rows)
            if depth > h:
                reduce_sent(1, bufs_b, (depth - h) * chunk)
                chunks_sent(1, ut, h + 1, depth - h)


def shards(right_sides, leaf_inverse, upper_inverse, leaf_update, upper_update, live_rows, tile_map):
    nl, nc = lax.axis_size("leaf"), lax.axis_size("col")
    depth = nl.bit_length() - 1
    _, rows, sn = leaf_inverse.shape
    width = right_sides.shape[3]
    anc, tile = tile_map.shape[2:]
    half, chunk = nc // 2, tile // nc
    up = max(depth - 1, 1)
    vm = lambda *shape: pltpu.VMEM(shape, BF16)
    four = lambda n: [vm(2, half, n, width)] + [vm(half, n, width)] * 3
    dma = lambda *shape: pltpu.SemaphoreType.DMA(shape)
    whole = pl.BlockSpec(memory_space=pltpu.VMEM)
    answer = pl.pallas_call(
        functools.partial(kernel, nl, nc, depth, anc),
        out_shape=jax.ShapeDtypeStruct((2, rows, width), BF16),
        in_specs=[whole] + [pl.BlockSpec(memory_space=pl.ANY)] * 4 + [pl.BlockSpec(memory_space=pltpu.SMEM), whole],
        out_specs=whole,
        scratch_shapes=[
            vm(rows, sn), vm(rows, sn), vm(depth, rows, tile), vm(up, rows, tile),
            vm(sn, rows), vm(sn, rows), vm(depth, tile, rows), vm(up, tile, rows),
            pltpu.VMEM((nl, 2 * anc, tile), jnp.int32),
            vm(nc, rows, width), vm(nc, rows, width), vm(depth, nc, rows, width),
            vm(depth, rows, sn), vm(up, rows, sn), vm(2, nl, rows, tile),
            vm(2, nl, nc, chunk, width), vm(rows, width), vm(rows, width),
            vm(depth, chunk, width), vm(up, chunk, width),
            pltpu.VMEM((rows, width), F32), pltpu.VMEM((rows, width), F32),
            *four(depth * chunk), *four(up * chunk), *four(rows), *four(rows),
            dma(nl), dma(nl),
            dma(depth + 2, half), dma(depth + 2, half), dma(depth + 2, nc),
            dma(4), dma(4), dma(4, half), dma(4, half),
            dma(2, depth, half), dma(2, nl, half), dma(2, nl, nc),
            dma(depth, nl), dma(depth), dma(4),
        ],
        compiler_params=pltpu.CompilerParams(has_side_effects=True, vmem_limit_bytes=56 * 1024 * 1024),
    )(
        right_sides[0], leaf_inverse[0], upper_inverse[0], leaf_update[0], upper_update[0],
        live_rows, tile_map[0].reshape(2 * anc, tile),
    )
    return answer[None]


def solution(mesh):
    placed = (
        P("leaf", None, "col", None),
        P("leaf", "col", None),
        P("leaf", "col", None),
        P("leaf", None, "col", None),
        P("leaf", None, "col", None),
        P("leaf", None),
        P("leaf", None, None, None),
    )
    return jax.shard_map(
        shards, mesh=mesh, in_specs=placed, out_specs=P("leaf", None, "col", None), check_vma=False
    )
```

```python
import functools

import jax
import jax.numpy as jnp
from jax import lax
from jax.experimental import pallas as pl
from jax.experimental.pallas import tpu as pltpu
from jax.sharding import PartitionSpec as P

MESH = pl.DeviceIdType.MESH
F32 = jnp.float32
BF16 = jnp.bfloat16


def dot(a, b, ca, cb):
    return lax.dot_general(a, b, (((ca,), (cb,)), ((), ())), preferred_element_type=F32)


def kernel(
    nl, nc, depth, anc, rs, linv_in, uinv_in, lupd_in, uupd_in, live, map_in, out,
    linv, uinv, lupd, uupd, linv_t, uinv_t, lupd_t, uupd_t,
    maps, rbuf, bbuf, xb, wl, wu, z_all, tiles, ylbuf, yubuf, lt, ut, b_sum, g_sum,
    a1, a2, a3, a4, b1, b2, b3, b4, c1, c2, c3, c4, d1, d2, d3, d4,
    map_send, map_recv, ag_send, ag_fwd, ag_recv, p_send, p_recv, q_send, q_recv,
    t_send, t_fwd, t_recv, x_send, x_recv, in_sem,
):
    rows, sn = linv.shape
    width = rs.shape[2]
    tile = map_in.shape[1]
    chunk = tile // nc
    half = nc // 2
    leaf = lax.axis_index("leaf")
    col = lax.axis_index("col")
    par = lax.rem(col, 2)
    z = lax.div(col, 2)
    sib = col + 1 - 2 * par
    level = jnp.int32(0)
    for k in range(depth):
        level = level + jnp.where((lax.rem(leaf, 2**k) == 0) & (leaf > 0), 1, 0)

    def base_of(h):
        return lax.div(leaf, 2**h) * 2**h

    def owner(h):
        return base_of(h) + 2 ** (h - 1)

    def rc(src, dst, send, recv, where, at=None):
        return pltpu.make_async_remote_copy(
            src_ref=src, dst_ref=dst, send_sem=send, recv_sem=recv,
            device_id=(leaf if at is None else at, where), device_id_type=MESH,
        )

    def got(ref, sem):
        rc(ref, ref, sem, sem, sib).wait_recv()

    def sent(ref, sem):
        rc(ref, ref, sem, sem, sib).wait_send()

    row_ids = col * rows + lax.broadcasted_iota(jnp.int32, (rows, width), 0)
    leaf_mask = row_ids < live[0, 0]
    upper_mask = row_ids < live[0, 1]

    def ag_start(use, buf):
        for k in range(1, half):
            to = 2 * lax.rem(z + k, half) + par
            rc(buf.at[col], buf.at[col], ag_send.at[use, k], ag_recv.at[use, col], to).start()
        rc(buf.at[col], buf.at[col], ag_send.at[use, 0], ag_recv.at[use, col], sib).start()

    def ag_forward(use, buf):
        for k in range(1, half):
            src = 2 * lax.rem(z - k + half, half) + par
            got(buf.at[src], ag_recv.at[use, src])
            rc(buf.at[src], buf.at[src], ag_fwd.at[use, k], ag_recv.at[use, src], sib).start()

    def ag_finish(use, buf):
        for zz in range(half):
            src = 2 * zz + 1 - par
            got(buf.at[src], ag_recv.at[use, src])

    def ag_sent(use, buf):
        for k in range(half):
            sent(buf.at[col], ag_send.at[use, k])
        for k in range(1, half):
            sent(buf.at[col], ag_fwd.at[use, k])

    def reduce(use, bufs, count):
        s1, r1, s2, r2 = bufs
        n = pl.ds(0, count)
        rc(s1.at[1 - par, :, n], r1.at[:, n], p_send.at[use, 0], p_recv.at[use, 0], sib).start()
        got(r1.at[:, n], p_recv.at[use, 0])
        for k in range(1, half):
            zz = lax.rem(z + k, half)
            s2[k, n] = (s1[par, zz, n].astype(F32) + r1[zz, n].astype(F32)).astype(BF16)
            rc(s2.at[k, n], r2.at[k, n], q_send.at[use, k], q_recv.at[use, k], 2 * zz + par).start()
        total = s1[par, z, n].astype(F32) + r1[z, n].astype(F32)
        for k in range(1, half):
            got(r2.at[k, n], q_recv.at[use, k])
            total = total + r2[k, n].astype(F32)
        return total

    def reduce_sent(use, bufs, count):
        s1, r1, s2, r2 = bufs
        n = pl.ds(0, count)
        sent(r1.at[:, n], p_send.at[use, 0])
        for k in range(1, half):
            sent(s2.at[k, n], q_send.at[use, k])

    def tile_parts(upd, slots, y, bufs):
        for s in range(slots):
            part = dot(upd[s], y, 1, 0).astype(BF16)
            for j in range(nc):
                bufs[0][j % 2, j // 2, s * chunk:(s + 1) * chunk] = part[j * chunk:(j + 1) * chunk]

    def send_chunks(which, held, first, slots):
        for s in range(slots):
            to = owner(first + s)
            for zz in range(half):

                @pl.when((to != leaf) | (z != zz))
                def _():
                    rc(held.at[s], tiles.at[which, leaf, col], t_send.at[which, s, zz],
                       t_recv.at[which, leaf, col], 2 * zz + par, to).start()

            @pl.when(to == leaf)
            def _():
                tiles[which, leaf, col] = held[s]

    def chunks_sent(which, held, first, slots):
        for s in range(slots):
            to = owner(first + s)
            for zz in range(half):

                @pl.when((to != leaf) | (z != zz))
                def _():
                    sent(held.at[s], t_send.at[which, s, zz])

    def onehot(row):
        ids = lax.broadcasted_iota(jnp.int32, (sn, tile), 0)
        return jnp.where(ids == row, 1.0, 0.0).astype(BF16)

    def stage(h):
        first = base_of(h)

        def level_in(i):
            out_level = jnp.int32(0)
            for k in range(depth):
                out_level = out_level + jnp.where((lax.rem(i, 2**k) == 0) & (i > 0), 1, 0)
            return out_level

        def each(fn):
            def leaf_body(i, _):
                fn(0, first + i, h - 1)
                return 0

            lax.fori_loop(0, 2**h, leaf_body, 0)
            if h > 1:

                def upper_body(i, _):
                    @pl.when(i != 2 ** (h - 1))
                    def _():
                        fn(1, first + i, anc + h - level_in(i) - 1)

                    return 0

                lax.fori_loop(1, 2**h, upper_body, 0)

        def prepare(which, src, slot):
            row = maps[src, pl.ds(slot, 1), :]
            row = jnp.where(row < live[0, 1], row, -1)
            z_all[which, src] = dot(uinv[...], onehot(row), 1, 0).astype(BF16)

        return each, prepare

    up = wu.shape[0]
    loads = [
        pltpu.make_async_copy(lupd_in.at[pl.ds(0, depth)], lupd, in_sem.at[0]),
        pltpu.make_async_copy(uinv_in, uinv, in_sem.at[1]),
        pltpu.make_async_copy(linv_in, linv, in_sem.at[2]),
        pltpu.make_async_copy(uupd_in.at[pl.ds(0, up)], uupd, in_sem.at[3]),
    ]
    for load in loads:
        load.start()
    rbuf[col] = jnp.where(leaf_mask, rs[0].astype(F32), 0.0).astype(BF16)
    ag_start(0, rbuf)
    bbuf[col] = jnp.where(upper_mask, rs[1].astype(F32), 0.0).astype(BF16)
    maps[leaf] = map_in[...]
    for k in range(1, nl):
        rc(maps.at[leaf], maps.at[leaf], map_send.at[k], map_recv.at[leaf], col, lax.rem(leaf + k, nl)).start()
    ag_forward(0, rbuf)
    loads[0].wait()
    for s in range(depth):
        lupd_t[s] = lupd[s].T
    for k in range(1, nl):
        src = lax.rem(leaf - k + nl, nl)
        got(maps.at[src], map_recv.at[src])
    loads[1].wait()
    for h in range(1, depth):

        @pl.when(level == h)
        def _():
            each, prepare = stage(h)
            each(prepare)

    loads[2].wait()
    loads[3].wait()
    ag_finish(0, rbuf)
    ag_start(1, bbuf)
    solved = dot(linv[...], rbuf[...].reshape(sn, width), 1, 0)
    ylbuf[...] = jnp.where(leaf_mask, solved, 0.0).astype(BF16)
    bufs_a, bufs_b, bufs_c, bufs_d = (a1, a2, a3, a4), (b1, b2, b3, b4), (c1, c2, c3, c4), (d1, d2, d3, d4)
    tile_parts(lupd_t, depth, ylbuf[...], bufs_a)
    lt[...] = reduce(0, bufs_a, depth * chunk).reshape(depth, chunk, width).astype(BF16)
    send_chunks(0, lt, 1, depth)
    ag_forward(1, bbuf)
    ag_finish(1, bbuf)
    yubuf[...] = jnp.zeros((rows, width), F32).astype(BF16)

    for h in range(1, depth + 1):

        @pl.when(level == h)
        def _():
            slots = depth - h
            each, prepare = stage(h)
            if h == depth:
                each(prepare)
                uinv_t[...] = uinv[...].T
            for s in range(slots):
                uupd_t[s] = uupd[s].T
            b_sum[...] = dot(uinv[...], bbuf[...].reshape(sn, width), 1, 0)

            def pass_on(which, src, slot):
                for zz in range(half):
                    c = 2 * zz + par

                    @pl.when((src != leaf) | (zz != z))
                    def _():
                        got(tiles.at[which, src, c], t_recv.at[which, src, c])

                    rc(tiles.at[which, src, c], tiles.at[which, src, c], t_fwd.at[which, src, zz],
                       t_recv.at[which, src, c], sib).start()

            def take(which, src, slot):
                for zz in range(half):
                    c = 2 * zz + 1 - par
                    got(tiles.at[which, src, c], t_recv.at[which, src, c])
                b_sum[...] -= dot(z_all[which, src], tiles[which, src].reshape(tile, width), 1, 0)

            each(pass_on)
            each(take)
            yubuf[...] = jnp.where(upper_mask, b_sum[...], 0.0).astype(BF16)
            if slots > 0:
                tile_parts(uupd_t, slots, yubuf[...], bufs_b)
                ut[pl.ds(0, slots)] = reduce(1, bufs_b, slots * chunk).reshape(slots, chunk, width).astype(BF16)
                send_chunks(1, ut, h + 1, slots)
                for s in range(slots):
                    wu[s] = dot(uupd[s], onehot(map_in[anc + s:anc + s + 1]), 1, 1).astype(BF16)
                uinv_t[...] = uinv[...].T

            def fwd_sent(which, src, slot):
                for zz in range(half):
                    sent(tiles.at[which, src, zz], t_fwd.at[which, src, zz])

            each(fwd_sent)

    def back(inv, y, g, mask, use, bufs):
        v = jnp.where(mask, y.astype(F32) - g, 0.0).astype(BF16)
        s1, r1, s2, r2 = bufs

        def block(zz, p):
            at = pl.multiple_of((2 * zz + p) * rows, 16)
            return dot(inv[pl.ds(at, rows), :], v, 1, 0)

        for k in [*range(1, half), 0]:
            zz = lax.rem(z + k, half)
            s1[1 - par, zz] = block(zz, 1 - par).astype(BF16)
            rc(s1.at[1 - par, zz], r1.at[zz], p_send.at[use, k], p_recv.at[use, k], sib).start()
        for k in range(1, half):
            zz = lax.rem(z + k, half)
            mine = block(zz, par)
            got(r1.at[zz], p_recv.at[use, k])
            s2[k] = (mine + r1[zz].astype(F32)).astype(BF16)
            rc(s2.at[k], r2.at[k], q_send.at[use, k], q_recv.at[use, k], 2 * zz + par).start()
        total = block(z, par)
        got(r1.at[z], p_recv.at[use, 0])
        total = total + r1[z].astype(F32)
        for k in range(1, half):
            got(r2.at[k], q_recv.at[use, k])
            total = total + r2[k].astype(F32)
        return jnp.where(mask, total, 0.0).astype(BF16)

    def back_sent(use, bufs):
        for k in range(half):
            sent(bufs[1].at[k], p_send.at[use, k])
        for k in range(1, half):
            sent(bufs[2].at[k], q_send.at[use, k])

    out[1] = jnp.zeros((rows, width), F32).astype(BF16)
    g_sum[...] = jnp.zeros((rows, width), F32)

    def ready():
        linv_t[...] = linv[...].T
        for s in range(depth):
            wl[s] = dot(lupd[s], onehot(map_in[s:s + 1]), 1, 1).astype(BF16)

    pl.when(level != depth)(ready)
    for h in range(depth, 0, -1):
        buf = xb.at[h - 1]

        @pl.when(level == h)
        def _():
            g = jnp.zeros((rows, width), F32)
            for s in range(depth - h):
                g = g + dot(wu[s], xb[h + s].reshape(sn, width), 1, 0)
            x = back(uinv_t, yubuf[...], g, upper_mask, 2, bufs_c)
            buf[col] = x
            for k in range(1, 2**h):
                to = base_of(h) + lax.rem(leaf - base_of(h) + k, 2**h)
                rc(buf.at[col], buf.at[col], x_send.at[h - 1, k], x_recv.at[h - 1], col, to).start()
            out[1] = x

        @pl.when(level != h)
        def _():
            got(buf.at[col], x_recv.at[h - 1])

        ag_start(1 + h, buf)
        ag_forward(1 + h, buf)
        ag_finish(1 + h, buf)
        if h == depth:
            pl.when(level == depth)(ready)
        if h > 1:
            g_sum[...] += dot(wl[h - 1], xb[h - 1].reshape(sn, width), 1, 0)
    g = g_sum[...] + dot(wl[0], xb[0].reshape(sn, width), 1, 0)
    out[0] = back(linv_t, ylbuf[...], g, leaf_mask, 3, bufs_d)

    for k in range(1, nl):
        sent(maps.at[leaf], map_send.at[k])
    ag_sent(0, rbuf)
    ag_sent(1, bbuf)
    reduce_sent(0, bufs_a, depth * chunk)
    back_sent(3, bufs_d)
    chunks_sent(0, lt, 1, depth)
    for h in range(1, depth + 1):
        buf = xb.at[h - 1]
        ag_sent(1 + h, buf)

        @pl.when(level == h)
        def _():
            for k in range(1, 2**h):
                sent(buf.at[col], x_send.at[h - 1, k])
            back_sent(2, bufs_c)
            if depth > h:
                reduce_sent(1, bufs_b, (depth - h) * chunk)
                chunks_sent(1, ut, h + 1, depth - h)


def shards(right_sides, leaf_inverse, upper_inverse, leaf_update, upper_update, live_rows, tile_map):
    nl, nc = lax.axis_size("leaf"), lax.axis_size("col")
    depth = nl.bit_length() - 1
    _, rows, sn = leaf_inverse.shape
    width = right_sides.shape[3]
    anc, tile = tile_map.shape[2:]
    half, chunk = nc // 2, tile // nc
    up = max(depth - 1, 1)
    vm = lambda *shape: pltpu.VMEM(shape, BF16)
    four = lambda n: [vm(2, half, n, width)] + [vm(half, n, width)] * 3
    dma = lambda *shape: pltpu.SemaphoreType.DMA(shape)
    whole = pl.BlockSpec(memory_space=pltpu.VMEM)
    answer = pl.pallas_call(
        functools.partial(kernel, nl, nc, depth, anc),
        out_shape=jax.ShapeDtypeStruct((2, rows, width), BF16),
        in_specs=[whole] + [pl.BlockSpec(memory_space=pl.ANY)] * 4 + [pl.BlockSpec(memory_space=pltpu.SMEM), whole],
        out_specs=whole,
        scratch_shapes=[
            vm(rows, sn), vm(rows, sn), vm(depth, rows, tile), vm(up, rows, tile),
            vm(sn, rows), vm(sn, rows), vm(depth, tile, rows), vm(up, tile, rows),
            pltpu.VMEM((nl, 2 * anc, tile), jnp.int32),
            vm(nc, rows, width), vm(nc, rows, width), vm(depth, nc, rows, width),
            vm(depth, rows, sn), vm(up, rows, sn), vm(2, nl, rows, tile),
            vm(2, nl, nc, chunk, width), vm(rows, width), vm(rows, width),
            vm(depth, chunk, width), vm(up, chunk, width),
            pltpu.VMEM((rows, width), F32), pltpu.VMEM((rows, width), F32),
            *four(depth * chunk), *four(up * chunk), *four(rows), *four(rows),
            dma(nl), dma(nl),
            dma(depth + 2, half), dma(depth + 2, half), dma(depth + 2, nc),
            dma(4, half), dma(4, half), dma(4, half), dma(4, half),
            dma(2, depth, half), dma(2, nl, half), dma(2, nl, nc),
            dma(depth, nl), dma(depth), dma(4),
        ],
        compiler_params=pltpu.CompilerParams(has_side_effects=True, vmem_limit_bytes=56 * 1024 * 1024),
    )(
        right_sides[0], leaf_inverse[0], upper_inverse[0], leaf_update[0], upper_update[0],
        live_rows, tile_map[0].reshape(2 * anc, tile),
    )
    return answer[None]


def solution(mesh):
    placed = (
        P("leaf", None, "col", None),
        P("leaf", "col", None),
        P("leaf", "col", None),
        P("leaf", None, "col", None),
        P("leaf", None, "col", None),
        P("leaf", None),
        P("leaf", None, None, None),
    )
    return jax.shard_map(
        shards, mesh=mesh, in_specs=placed, out_specs=P("leaf", None, "col", None), check_vma=False
    )
```

```python
import functools

import jax
import jax.numpy as jnp
from jax import lax
from jax.experimental import pallas as pl
from jax.experimental.pallas import tpu as pltpu
from jax.sharding import PartitionSpec as P

MESH = pl.DeviceIdType.MESH
F32 = jnp.float32
BF16 = jnp.bfloat16


def dot(a, b, ca, cb):
    return lax.dot_general(a, b, (((ca,), (cb,)), ((), ())), preferred_element_type=F32)


def kernel(
    nl, nc, depth, anc, rs, linv_in, uinv_in, lupd_in, uupd_in, live, map_in, out,
    linv, uinv, lupd, uupd, linv_t, uinv_t, lupd_t, uupd_t,
    maps, rbuf, bbuf, xb, wl, wu, z_all, tiles, ylbuf, yubuf, lt, ut, b_sum, g_sum,
    a1, a2, a3, a4, b1, b2, b3, b4, c1, c2, c3, c4, d1, d2, d3, d4,
    map_send, map_recv, ag_send, ag_fwd, ag_recv, p_send, p_recv, q_send, q_recv,
    t_send, t_fwd, t_recv, x_send, x_recv, in_sem,
):
    rows, sn = linv.shape
    width = rs.shape[2]
    tile = map_in.shape[1]
    chunk = tile // nc
    half = nc // 2
    leaf = lax.axis_index("leaf")
    col = lax.axis_index("col")
    par = lax.rem(col, 2)
    z = lax.div(col, 2)
    sib = col + 1 - 2 * par
    level = jnp.int32(0)
    for k in range(depth):
        level = level + jnp.where((lax.rem(leaf, 2**k) == 0) & (leaf > 0), 1, 0)

    def base_of(h):
        return lax.div(leaf, 2**h) * 2**h

    def owner(h):
        return base_of(h) + 2 ** (h - 1)

    def rc(src, dst, send, recv, where, at=None):
        return pltpu.make_async_remote_copy(
            src_ref=src, dst_ref=dst, send_sem=send, recv_sem=recv,
            device_id=(leaf if at is None else at, where), device_id_type=MESH,
        )

    def got(ref, sem):
        rc(ref, ref, sem, sem, sib).wait_recv()

    def sent(ref, sem):
        rc(ref, ref, sem, sem, sib).wait_send()

    row_ids = col * rows + lax.broadcasted_iota(jnp.int32, (rows, width), 0)
    leaf_mask = row_ids < live[0, 0]
    upper_mask = row_ids < live[0, 1]

    def ag_start(use, buf):
        rc(buf.at[col], buf.at[col], ag_send.at[use, 0], ag_recv.at[use, col], sib).start()
        for k in range(1, half):
            to = 2 * lax.rem(z + k, half) + par
            rc(buf.at[col], buf.at[col], ag_send.at[use, k], ag_recv.at[use, col], to).start()

    def ag_forward(use, buf):
        for k in range(1, half):
            src = 2 * lax.rem(z - k + half, half) + par
            got(buf.at[src], ag_recv.at[use, src])
            rc(buf.at[src], buf.at[src], ag_fwd.at[use, k], ag_recv.at[use, src], sib).start()

    def ag_finish(use, buf):
        for zz in range(half):
            src = 2 * zz + 1 - par
            got(buf.at[src], ag_recv.at[use, src])

    def ag_sent(use, buf):
        for k in range(half):
            sent(buf.at[col], ag_send.at[use, k])
        for k in range(1, half):
            sent(buf.at[col], ag_fwd.at[use, k])

    def reduce(use, bufs, count):
        s1, r1, s2, r2 = bufs
        n = pl.ds(0, count)
        rc(s1.at[1 - par, :, n], r1.at[:, n], p_send.at[use, 0], p_recv.at[use, 0], sib).start()
        got(r1.at[:, n], p_recv.at[use, 0])
        for k in range(1, half):
            zz = lax.rem(z + k, half)
            s2[k, n] = (s1[par, zz, n].astype(F32) + r1[zz, n].astype(F32)).astype(BF16)
            rc(s2.at[k, n], r2.at[k, n], q_send.at[use, k], q_recv.at[use, k], 2 * zz + par).start()
        total = s1[par, z, n].astype(F32) + r1[z, n].astype(F32)
        for k in range(1, half):
            got(r2.at[k, n], q_recv.at[use, k])
            total = total + r2[k, n].astype(F32)
        return total

    def reduce_sent(use, bufs, count):
        s1, r1, s2, r2 = bufs
        n = pl.ds(0, count)
        sent(r1.at[:, n], p_send.at[use, 0])
        for k in range(1, half):
            sent(s2.at[k, n], q_send.at[use, k])

    def tile_parts(upd, slots, y, bufs):
        for s in range(slots):
            part = dot(upd[s], y, 1, 0).astype(BF16)
            for j in range(nc):
                bufs[0][j % 2, j // 2, s * chunk:(s + 1) * chunk] = part[j * chunk:(j + 1) * chunk]

    def send_chunks(which, held, first, slots):
        for s in range(slots):
            to = owner(first + s)
            for zz in range(half):

                @pl.when((to != leaf) | (z != zz))
                def _():
                    rc(held.at[s], tiles.at[which, leaf, col], t_send.at[which, s, zz],
                       t_recv.at[which, leaf, col], 2 * zz + par, to).start()

            @pl.when(to == leaf)
            def _():
                tiles[which, leaf, col] = held[s]

    def chunks_sent(which, held, first, slots):
        for s in range(slots):
            to = owner(first + s)
            for zz in range(half):

                @pl.when((to != leaf) | (z != zz))
                def _():
                    sent(held.at[s], t_send.at[which, s, zz])

    def onehot(row):
        ids = lax.broadcasted_iota(jnp.int32, (sn, tile), 0)
        return jnp.where(ids == row, 1.0, 0.0).astype(BF16)

    def stage(h):
        first = base_of(h)

        def level_in(i):
            out_level = jnp.int32(0)
            for k in range(depth):
                out_level = out_level + jnp.where((lax.rem(i, 2**k) == 0) & (i > 0), 1, 0)
            return out_level

        def each(fn):
            def leaf_body(i, _):
                fn(0, first + i, h - 1)
                return 0

            lax.fori_loop(0, 2**h, leaf_body, 0)
            if h > 1:

                def upper_body(i, _):
                    @pl.when(i != 2 ** (h - 1))
                    def _():
                        fn(1, first + i, anc + h - level_in(i) - 1)

                    return 0

                lax.fori_loop(1, 2**h, upper_body, 0)

        def prepare(which, src, slot):
            row = maps[src, pl.ds(slot, 1), :]
            row = jnp.where(row < live[0, 1], row, -1)
            z_all[which, src] = dot(uinv[...], onehot(row), 1, 0).astype(BF16)

        return each, prepare

    up = wu.shape[0]
    loads = [
        pltpu.make_async_copy(lupd_in.at[pl.ds(0, depth)], lupd, in_sem.at[0]),
        pltpu.make_async_copy(uinv_in, uinv, in_sem.at[1]),
        pltpu.make_async_copy(linv_in, linv, in_sem.at[2]),
        pltpu.make_async_copy(uupd_in.at[pl.ds(0, up)], uupd, in_sem.at[3]),
    ]
    for load in loads:
        load.start()
    rbuf[col] = jnp.where(leaf_mask, rs[0].astype(F32), 0.0).astype(BF16)
    ag_start(0, rbuf)
    bbuf[col] = jnp.where(upper_mask, rs[1].astype(F32), 0.0).astype(BF16)
    ag_start(1, bbuf)
    maps[leaf] = map_in[...]
    for k in range(1, nl):
        rc(maps.at[leaf], maps.at[leaf], map_send.at[k], map_recv.at[leaf], col, lax.rem(leaf + k, nl)).start()
    ag_forward(0, rbuf)
    loads[0].wait()
    for s in range(depth):
        lupd_t[s] = lupd[s].T
    for k in range(1, nl):
        src = lax.rem(leaf - k + nl, nl)
        got(maps.at[src], map_recv.at[src])
    loads[1].wait()
    for h in range(1, depth):

        @pl.when(level == h)
        def _():
            each, prepare = stage(h)
            each(prepare)

    loads[2].wait()
    loads[3].wait()
    ag_finish(0, rbuf)
    solved = dot(linv[...], rbuf[...].reshape(sn, width), 1, 0)
    ylbuf[...] = jnp.where(leaf_mask, solved, 0.0).astype(BF16)
    bufs_a, bufs_b, bufs_c, bufs_d = (a1, a2, a3, a4), (b1, b2, b3, b4), (c1, c2, c3, c4), (d1, d2, d3, d4)
    tile_parts(lupd_t, depth, ylbuf[...], bufs_a)
    lt[...] = reduce(0, bufs_a, depth * chunk).reshape(depth, chunk, width).astype(BF16)
    send_chunks(0, lt, 1, depth)
    ag_forward(1, bbuf)
    ag_finish(1, bbuf)
    yubuf[...] = jnp.zeros((rows, width), F32).astype(BF16)

    for h in range(1, depth + 1):

        @pl.when(level == h)
        def _():
            slots = depth - h
            each, prepare = stage(h)
            if h == depth:
                each(prepare)
                uinv_t[...] = uinv[...].T
            for s in range(slots):
                uupd_t[s] = uupd[s].T
            b_sum[...] = dot(uinv[...], bbuf[...].reshape(sn, width), 1, 0)

            def pass_on(which, src, slot):
                for zz in range(half):
                    c = 2 * zz + par

                    @pl.when((src != leaf) | (zz != z))
                    def _():
                        got(tiles.at[which, src, c], t_recv.at[which, src, c])

                    rc(tiles.at[which, src, c], tiles.at[which, src, c], t_fwd.at[which, src, zz],
                       t_recv.at[which, src, c], sib).start()

            def take(which, src, slot):
                for zz in range(half):
                    c = 2 * zz + 1 - par
                    got(tiles.at[which, src, c], t_recv.at[which, src, c])
                b_sum[...] -= dot(z_all[which, src], tiles[which, src].reshape(tile, width), 1, 0)

            each(pass_on)
            each(take)
            yubuf[...] = jnp.where(upper_mask, b_sum[...], 0.0).astype(BF16)
            if slots > 0:
                tile_parts(uupd_t, slots, yubuf[...], bufs_b)
                ut[pl.ds(0, slots)] = reduce(1, bufs_b, slots * chunk).reshape(slots, chunk, width).astype(BF16)
                send_chunks(1, ut, h + 1, slots)
                for s in range(slots):
                    wu[s] = dot(uupd[s], onehot(map_in[anc + s:anc + s + 1]), 1, 1).astype(BF16)
                uinv_t[...] = uinv[...].T

            def fwd_sent(which, src, slot):
                for zz in range(half):
                    sent(tiles.at[which, src, zz], t_fwd.at[which, src, zz])

            each(fwd_sent)

    def back(inv, y, g, mask, use, bufs):
        v = jnp.where(mask, y.astype(F32) - g, 0.0).astype(BF16)
        s1, r1, s2, r2 = bufs

        def block(zz, p):
            at = pl.multiple_of((2 * zz + p) * rows, 16)
            return dot(inv[pl.ds(at, rows), :], v, 1, 0)

        for k in [*range(1, half), 0]:
            zz = lax.rem(z + k, half)
            s1[1 - par, zz] = block(zz, 1 - par).astype(BF16)
            rc(s1.at[1 - par, zz], r1.at[zz], p_send.at[use, k], p_recv.at[use, k], sib).start()
        for k in range(1, half):
            zz = lax.rem(z + k, half)
            mine = block(zz, par)
            got(r1.at[zz], p_recv.at[use, k])
            s2[k] = (mine + r1[zz].astype(F32)).astype(BF16)
            rc(s2.at[k], r2.at[k], q_send.at[use, k], q_recv.at[use, k], 2 * zz + par).start()
        total = block(z, par)
        got(r1.at[z], p_recv.at[use, 0])
        total = total + r1[z].astype(F32)
        for k in range(1, half):
            got(r2.at[k], q_recv.at[use, k])
            total = total + r2[k].astype(F32)
        return jnp.where(mask, total, 0.0).astype(BF16)

    def back_sent(use, bufs):
        for k in range(half):
            sent(bufs[1].at[k], p_send.at[use, k])
        for k in range(1, half):
            sent(bufs[2].at[k], q_send.at[use, k])

    out[1] = jnp.zeros((rows, width), F32).astype(BF16)
    g_sum[...] = jnp.zeros((rows, width), F32)

    def ready():
        linv_t[...] = linv[...].T
        for s in range(depth):
            wl[s] = dot(lupd[s], onehot(map_in[s:s + 1]), 1, 1).astype(BF16)

    pl.when(level != depth)(ready)
    for h in range(depth, 0, -1):
        buf = xb.at[h - 1]

        @pl.when(level == h)
        def _():
            g = jnp.zeros((rows, width), F32)
            for s in range(depth - h):
                g = g + dot(wu[s], xb[h + s].reshape(sn, width), 1, 0)
            x = back(uinv_t, yubuf[...], g, upper_mask, 2, bufs_c)
            buf[col] = x
            for k in range(1, 2**h):
                to = base_of(h) + lax.rem(leaf - base_of(h) + k, 2**h)
                rc(buf.at[col], buf.at[col], x_send.at[h - 1, k], x_recv.at[h - 1], col, to).start()
            out[1] = x

        @pl.when(level != h)
        def _():
            got(buf.at[col], x_recv.at[h - 1])

        ag_start(1 + h, buf)
        ag_forward(1 + h, buf)
        ag_finish(1 + h, buf)
        if h == depth:
            pl.when(level == depth)(ready)
        if h > 1:
            g_sum[...] += dot(wl[h - 1], xb[h - 1].reshape(sn, width), 1, 0)
    g = g_sum[...] + dot(wl[0], xb[0].reshape(sn, width), 1, 0)
    out[0] = back(linv_t, ylbuf[...], g, leaf_mask, 3, bufs_d)

    for k in range(1, nl):
        sent(maps.at[leaf], map_send.at[k])
    ag_sent(0, rbuf)
    ag_sent(1, bbuf)
    reduce_sent(0, bufs_a, depth * chunk)
    back_sent(3, bufs_d)
    chunks_sent(0, lt, 1, depth)
    for h in range(1, depth + 1):
        buf = xb.at[h - 1]
        ag_sent(1 + h, buf)

        @pl.when(level == h)
        def _():
            for k in range(1, 2**h):
                sent(buf.at[col], x_send.at[h - 1, k])
            back_sent(2, bufs_c)
            if depth > h:
                reduce_sent(1, bufs_b, (depth - h) * chunk)
                chunks_sent(1, ut, h + 1, depth - h)


def shards(right_sides, leaf_inverse, upper_inverse, leaf_update, upper_update, live_rows, tile_map):
    nl, nc = lax.axis_size("leaf"), lax.axis_size("col")
    depth = nl.bit_length() - 1
    _, rows, sn = leaf_inverse.shape
    width = right_sides.shape[3]
    anc, tile = tile_map.shape[2:]
    half, chunk = nc // 2, tile // nc
    up = max(depth - 1, 1)
    vm = lambda *shape: pltpu.VMEM(shape, BF16)
    four = lambda n: [vm(2, half, n, width)] + [vm(half, n, width)] * 3
    dma = lambda *shape: pltpu.SemaphoreType.DMA(shape)
    whole = pl.BlockSpec(memory_space=pltpu.VMEM)
    answer = pl.pallas_call(
        functools.partial(kernel, nl, nc, depth, anc),
        out_shape=jax.ShapeDtypeStruct((2, rows, width), BF16),
        in_specs=[whole] + [pl.BlockSpec(memory_space=pl.ANY)] * 4 + [pl.BlockSpec(memory_space=pltpu.SMEM), whole],
        out_specs=whole,
        scratch_shapes=[
            vm(rows, sn), vm(rows, sn), vm(depth, rows, tile), vm(up, rows, tile),
            vm(sn, rows), vm(sn, rows), vm(depth, tile, rows), vm(up, tile, rows),
            pltpu.VMEM((nl, 2 * anc, tile), jnp.int32),
            vm(nc, rows, width), vm(nc, rows, width), vm(depth, nc, rows, width),
            vm(depth, rows, sn), vm(up, rows, sn), vm(2, nl, rows, tile),
            vm(2, nl, nc, chunk, width), vm(rows, width), vm(rows, width),
            vm(depth, chunk, width), vm(up, chunk, width),
            pltpu.VMEM((rows, width), F32), pltpu.VMEM((rows, width), F32),
            *four(depth * chunk), *four(up * chunk), *four(rows), *four(rows),
            dma(nl), dma(nl),
            dma(depth + 2, half), dma(depth + 2, half), dma(depth + 2, nc),
            dma(4, half), dma(4, half), dma(4, half), dma(4, half),
            dma(2, depth, half), dma(2, nl, half), dma(2, nl, nc),
            dma(depth, nl), dma(depth), dma(4),
        ],
        compiler_params=pltpu.CompilerParams(has_side_effects=True, vmem_limit_bytes=56 * 1024 * 1024),
    )(
        right_sides[0], leaf_inverse[0], upper_inverse[0], leaf_update[0], upper_update[0],
        live_rows, tile_map[0].reshape(2 * anc, tile),
    )
    return answer[None]


def solution(mesh):
    placed = (
        P("leaf", None, "col", None),
        P("leaf", "col", None),
        P("leaf", "col", None),
        P("leaf", None, "col", None),
        P("leaf", None, "col", None),
        P("leaf", None),
        P("leaf", None, None, None),
    )
    return jax.shard_map(
        shards, mesh=mesh, in_specs=placed, out_specs=P("leaf", None, "col", None), check_vma=False
    )
```
